32 devices in a mesh: seq: 8 (over z, x), batch: 4 (over y, core).
Axes of the slice: x: 2, y: 2, z: 4, core: 2. Of those that a mesh axis runs over, the one named last changes fastest.
Arguments:
- signal: bfloat16 [65536, 512], P(('batch', 'seq')), parts along dimension 0, may hold values from -6 to 6
- kernel_weight_stack: bfloat16 [2, 1024, 1024], P(None, 'seq'), may hold values from -0.1875 to 0.1875
- blend_weight_stack: bfloat16 [2, 512, 512], P(None, 'seq'), may hold values from -0.25 to 0.25
Outputs:
- layer_outs: bfloat16 [2, 65536, 512], P(None, ('batch', 'seq')), parts along dimension 1
The draws below stay inside these ranges and needn't reach their ends.
There are 4 independent parts, one for each index of `batch`. The reference program is written for one: setup_inputs(seed, part) draws one part's arguments, and reference() takes and returns one part's arrays. A program takes and returns all parts, laid end to end along the dimension named above; an argument that names none is the same for every part. Nothing has to cross between parts.
All inputs are finite; a program needn't handle non-finite values.
Results may differ from the reference program's by a relative error of at most 0.0043.
Values may be sent and summed in bfloat16 or wider, within the bound.
A program may use at most 64 MiB of HBM per device.

```python
import jax
import jax.numpy as jnp

C = 512
LAYERS = 2
FIRST_SPACING = 1024
LENGTH = 16384


def levels(own_key, shape, pieces, smallest, largest):
    factor_of = 1.0
    for axis_at, parts in pieces:
        heights = jax.random.uniform(jax.random.fold_in(jax.random.fold_in(own_key, 6), axis_at), (parts,), jnp.float32, smallest / len(pieces), largest / len(pieces))
        factor_of = factor_of * jnp.repeat(jnp.exp(heights), shape[axis_at] // parts).reshape((-1,) + (1,) * (len(shape) - 1 - axis_at))
    return factor_of


def normal_values(own_key, shape, spread, reach, pieces=(), dtype=jnp.bfloat16):
    array = spread * jax.random.normal(own_key, shape, jnp.float32)
    if pieces:
        array = array * levels(own_key, shape, pieces, -0.22, 0.18)
    return jnp.clip(array, -reach, reach).astype(dtype)


def setup_inputs(seed: int = 0, part: int = 0) -> dict:
    seeds = jax.random.split(jax.random.key(seed), 4)
    own_keys = jax.random.split(jax.random.fold_in(seeds[3], part), 4)
    return {
        "signal": normal_values(own_keys[0], (LENGTH, C), 1.0, 6.0, ((0, 8),)),
        "kernel_weight_stack": normal_values(seeds[1], (LAYERS, 2 * C, 2 * C), (2 * C) ** -0.5, 0.1875, ((1, 8),)),
        "blend_weight_stack": normal_values(seeds[2], (LAYERS, C, C), C ** -0.5, 0.25, ((1, 8),)),
    }


def reference(signal, kernel_weight_stack, blend_weight_stack):
    hidden = signal
    layer_outs = []
    for layer_position_index in range(LAYERS):
        layer_spacing = FIRST_SPACING * (2 ** layer_position_index)
        if layer_spacing < LENGTH:
            delayed = jnp.concatenate([jnp.zeros((layer_spacing, C), jnp.bfloat16), hidden[:LENGTH - layer_spacing]], axis=0)
        else:
            delayed = jnp.zeros_like(hidden)
        stacked_in = jnp.concatenate([delayed, hidden], axis=1)
        preact = jnp.dot(stacked_in, kernel_weight_stack[layer_position_index], preferred_element_type=jnp.float32)
        gated_output = (jnp.tanh(preact[:, :C]) * jax.nn.sigmoid(preact[:, C:])).astype(jnp.bfloat16)
        mix_out = jnp.dot(gated_output, blend_weight_stack[layer_position_index], preferred_element_type=jnp.float32)
        hidden = (hidden.astype(jnp.float32) + mix_out).astype(jnp.bfloat16)
        layer_outs.append(hidden)
    return jnp.stack(layer_outs)
```

```python
import functools

import jax
import jax.numpy as jnp
from jax import lax
from jax.experimental import pallas as pl
from jax.experimental.pallas import tpu as pltpu
from jax.sharding import PartitionSpec as P

MESH = pl.DeviceIdType.MESH
TILE = 256


def flip(index, bit):
    return index + bit - 2 * bit * ((index // bit) % 2)


def kernel(n, nb, gather_blend, sig, kw, bw, out, sbuf, hbuf, obuf, kfull, bfull,
           seq_s, seq_r, bat_s, bat_r, act_s, act_r, own_sem, load_sem, out_sem):
    i = lax.axis_index("seq")
    b = lax.axis_index("batch")
    rows = sig.shape[0]
    half = rows // 2
    layers = kw.shape[0]
    channels = sig.shape[1]
    masks = [nb >> (k + 1) for k in range(nb.bit_length() - 1)]

    load = pltpu.make_async_copy(sig, sbuf.at[pl.ds(3 * half, rows)], load_sem)
    load.start()

    barrier = pltpu.get_barrier_semaphore()

    def greet(d, _):
        pl.semaphore_signal(barrier, inc=1, device_id={"seq": lax.rem(i + d, n)}, device_id_type=MESH)
        return 0

    lax.fori_loop(1, n, greet, 0)
    for m in masks:
        pl.semaphore_signal(barrier, inc=1, device_id={"batch": flip(b, m)}, device_id_type=MESH)

    weights = [(kw, kfull)] + ([(bw, bfull)] if gather_blend else [])

    def cols(full, quarter):
        width = full.shape[2] // nb
        return pl.ds(pl.multiple_of(quarter * width, width), width)

    def shard(full, part, l, source, quarter):
        count = part.shape[1]
        return full.at[l, pl.ds(pl.multiple_of(source * count, count), count), cols(full, quarter)]

    def seq_copy(l, w, d):
        part, full = weights[w]
        return pltpu.make_async_remote_copy(
            src_ref=part.at[l, :, cols(full, b)],
            dst_ref=shard(full, part, l, i, b),
            send_sem=seq_s.at[l, w, d], recv_sem=seq_r.at[l, w, d],
            device_id={"seq": lax.rem(i + d, n)}, device_id_type=MESH)

    def own_copy(l, w):
        part, full = weights[w]
        return pltpu.make_async_copy(part.at[l, :, cols(full, b)], shard(full, part, l, i, b), own_sem.at[l, w])

    def bat_copy(l, w, m, o):
        part, full = weights[w]
        quarter = b
        for bit in masks:
            if o & bit:
                quarter = flip(quarter, bit)
        where = full.at[l, :, cols(full, quarter)]
        return pltpu.make_async_remote_copy(
            src_ref=where, dst_ref=where,
            send_sem=bat_s.at[l, w, o + m], recv_sem=bat_r.at[l, w, o + m],
            device_id={"batch": flip(b, m)}, device_id_type=MESH)

    def act_copy(k):
        source, slot, hop = ((half, 2, 1), (0, 1, 1), (half, 0, 2))[k]
        return hop, pltpu.make_async_remote_copy(
            src_ref=sig.at[pl.ds(source, half)], dst_ref=sbuf.at[pl.ds(slot * half, half)],
            send_sem=act_s.at[k], recv_sem=act_r.at[k],
            device_id={"seq": lax.rem(i + hop, n)}, device_id_type=MESH)

    def seq_start(l):
        def go(d, _):
            for w in range(len(weights)):
                seq_copy(l, w, d).start()
            return 0
        lax.fori_loop(1, n, go, 0)

    def seq_wait(l):
        def go(d, _):
            for w in range(len(weights)):
                seq_copy(l, w, d).wait_recv()
            return 0
        lax.fori_loop(1, n, go, 0)
        for w in range(len(weights)):
            own_copy(l, w).wait()

    for l in range(layers):
        for w in range(len(weights)):
            own_copy(l, w).start()
    if not gather_blend:
        blend = pltpu.make_async_copy(bw, bfull, own_sem.at[0, 1])
        blend.start()

    pl.semaphore_wait(barrier, n - 1 + len(masks))
    seq_start(0)
    for k in range(3):
        hop, copy = act_copy(k)
        pl.when(i + hop < n)(copy.start)
        pl.when(i < hop)(functools.partial(zero, sbuf, ((2, 1, 0)[k]) * half, half))
    seq_start(1)

    stages = [(m, [o for o in range(nb) if o % (2 * m) == 0 and all(o & x == 0 or x > m for x in masks)])
              for m in masks]

    def bat_start(l, s):
        m, held = stages[s]
        for o in held:
            for w in range(len(weights)):
                bat_copy(l, w, m, o).start()

    def bat_wait(l, s):
        m, held = stages[s]
        for o in held:
            for w in range(len(weights)):
                bat_copy(l, w, m, o).wait_recv()

    def layer(l, src, dst, shift, start, keep):
        def tile(t, _):
            at = pl.multiple_of(start + t * TILE, TILE)
            now = src[pl.ds(at + shift, TILE), :]
            late = src[pl.ds(at, TILE), :]
            pre = jnp.dot(late, kfull[l, :channels, :], preferred_element_type=jnp.float32)
            pre += jnp.dot(now, kfull[l, channels:, :], preferred_element_type=jnp.float32)
            gate = 0.5 * jnp.tanh(0.5 * pre[:, channels:]) + 0.5
            gated = (jnp.tanh(pre[:, :channels]) * gate).astype(jnp.bfloat16)
            mix = jnp.dot(gated, bfull[l], preferred_element_type=jnp.float32)
            dst[pl.ds(at, TILE), :] = (now.astype(jnp.float32) + mix).astype(jnp.bfloat16)
            return 0
        lax.fori_loop(0, half // TILE, tile, 0, unroll=2)
        if keep is not None:
            copy = pltpu.make_async_copy(
                dst.at[pl.ds(start, half)], out.at[l, pl.ds(keep * half, half)], out_sem.at[l, keep])
            copy.start()
            return [copy]
        return []

    def act_wait(k):
        hop, copy = act_copy(k)
        pl.when(i >= hop)(copy.wait_recv)

    seq_wait(0)
    for s in range(len(stages)):
        bat_start(0, s)
        bat_wait(0, s)
    load.wait()
    if not gather_blend:
        blend.wait()
    done = layer(0, sbuf, hbuf, half, 3 * half, 1)
    seq_wait(1)
    bat_start(1, 0)
    act_wait(0)
    done += layer(0, sbuf, hbuf, half, 2 * half, 0)
    for s in range(1, len(stages)):
        bat_wait(1, s - 1)
        bat_start(1, s)
    act_wait(1)
    done += layer(0, sbuf, hbuf, half, half, None)
    bat_wait(1, len(stages) - 1)
    done += layer(1, hbuf, obuf, rows, half, 1)
    act_wait(2)
    done += layer(0, sbuf, hbuf, half, 0, None)
    done += layer(1, hbuf, obuf, rows, 0, 0)

    def seq_sent(d, _):
        for l in range(layers):
            for w in range(len(weights)):
                seq_copy(l, w, d).wait_send()
        return 0

    lax.fori_loop(1, n, seq_sent, 0)
    for l in range(layers):
        for m, held in stages:
            for o in held:
                for w in range(len(weights)):
                    bat_copy(l, w, m, o).wait_send()
    for k in range(3):
        hop, copy = act_copy(k)
        pl.when(i + hop < n)(copy.wait_send)
    for copy in done:
        copy.wait()


def zero(ref, start, count):
    ref[pl.ds(start, count), :] = jnp.zeros((count, ref.shape[1]), ref.dtype)


def per_device(n, nb, signal, kernel_weight_stack, blend_weight_stack):
    rows, channels = signal.shape
    layers, part_rows, width = kernel_weight_stack.shape
    gather_blend = blend_weight_stack.shape[1] % 16 == 0
    if not gather_blend:
        blend_weight_stack = lax.all_gather(blend_weight_stack, "seq", axis=1, tiled=True)
    half = rows // 2
    dma = pltpu.SemaphoreType.DMA
    any_space = pl.BlockSpec(memory_space=pl.ANY)
    return pl.pallas_call(
        functools.partial(kernel, n, nb, gather_blend),
        out_shape=jax.ShapeDtypeStruct((layers, rows, channels), signal.dtype),
        in_specs=[any_space] * 3,
        out_specs=any_space,
        scratch_shapes=[
            pltpu.VMEM((5 * half, channels), signal.dtype),
            pltpu.VMEM((4 * half, channels), signal.dtype),
            pltpu.VMEM((rows, channels), signal.dtype),
            pltpu.VMEM((layers, n * part_rows, width), signal.dtype),
            pltpu.VMEM((layers, channels, channels), signal.dtype),
            dma((layers, 2, n)), dma((layers, 2, n)),
            dma((layers, 2, nb)), dma((layers, 2, nb)),
            dma((3,)), dma((3,)),
            dma((layers, 2)), dma, dma((layers, 2)),
        ],
        compiler_params=pltpu.CompilerParams(
            collective_id=0, has_side_effects=True, vmem_limit_bytes=48 * 2**20),
        cost_estimate=pl.CostEstimate(
            flops=3 * 2 * rows * channels * (2 * width + channels),
            bytes_accessed=2 * rows * channels * 2 * 3, transcendentals=3 * rows * width),
    )(signal, kernel_weight_stack, blend_weight_stack)


def solution(mesh):
    return jax.shard_map(
        functools.partial(per_device, mesh.shape["seq"], mesh.shape["batch"]),
        mesh=mesh,
        in_specs=(P(("batch", "seq"), None), P(None, "seq", None), P(None, "seq", None)),
        out_specs=P(None, ("batch", "seq"), None),
        check_vma=False,
    )
```

```python
import functools

import jax
import jax.numpy as jnp
from jax import lax
from jax.experimental import pallas as pl
from jax.experimental.pallas import tpu as pltpu
from jax.sharding import PartitionSpec as P

MESH = pl.DeviceIdType.MESH
TILE = 256
CHUNKS = 2


def flip(index, bit):
    return index + bit - 2 * bit * ((index // bit) % 2)


def kernel(n, nb, gather_blend, sig, kw, bw, out, sbuf, hbuf, obuf, kfull, bfull,
           seq_s, seq_r, par_s, par_r, bat_s, bat_r, act_s, act_r, own_sem, load_sem, out_sem):
    i = lax.axis_index("seq")
    b = lax.axis_index("batch")
    rows = sig.shape[0]
    half = rows // 2
    chunk = half // CHUNKS
    layers = kw.shape[0]
    channels = sig.shape[1]
    masks = [nb >> (k + 1) for k in range(nb.bit_length() - 1)]
    pairs = n // 2
    pair, side = i // 2, i % 2
    partner = flip(i, 1)

    load = pltpu.make_async_copy(sig, sbuf.at[pl.ds(3 * half, rows)], load_sem)
    load.start()

    barrier = pltpu.get_barrier_semaphore()

    def greet(d, _):
        pl.semaphore_signal(barrier, inc=1, device_id={"seq": lax.rem(i + d, n)}, device_id_type=MESH)
        return 0

    lax.fori_loop(1, n, greet, 0)
    for m in masks:
        pl.semaphore_signal(barrier, inc=1, device_id={"batch": flip(b, m)}, device_id_type=MESH)

    weights = [(kw, kfull)] + ([(bw, bfull)] if gather_blend else [])
    both = range(len(weights))

    def cols(full, quarter):
        width = full.shape[-1] // nb
        return pl.ds(pl.multiple_of(quarter * width, width), width)

    def seq_copy(l, w, d):
        part, full = weights[w]
        return pltpu.make_async_remote_copy(
            src_ref=part.at[l, :, cols(full, b)],
            dst_ref=full.at[l, pair, side, :, cols(full, b)],
            send_sem=seq_s.at[l, w, d], recv_sem=seq_r.at[l, w, d],
            device_id={"seq": lax.rem(i + 2 * d, n)}, device_id_type=MESH)

    def own_copy(l, w):
        part, full = weights[w]
        return pltpu.make_async_copy(
            part.at[l, :, cols(full, b)], full.at[l, pair, side, :, cols(full, b)], own_sem.at[l, w])

    def par_copy(l, w):
        part, full = weights[w]
        where = full.at[l, :, side, :, cols(full, b)]
        return pltpu.make_async_remote_copy(
            src_ref=where, dst_ref=where, send_sem=par_s.at[l, w], recv_sem=par_r.at[l, w],
            device_id={"seq": partner}, device_id_type=MESH)

    def bat_copy(l, w, m, o, parity):
        part, full = weights[w]
        quarter = b
        for bit in masks:
            if o & bit:
                quarter = flip(quarter, bit)
        which = lax.rem(side + parity, 2)
        where = full.at[l, :, which, :, cols(full, quarter)]
        return pltpu.make_async_remote_copy(
            src_ref=where, dst_ref=where,
            send_sem=bat_s.at[l, w, o + m, parity], recv_sem=bat_r.at[l, w, o + m, parity],
            device_id={"batch": flip(b, m)}, device_id_type=MESH)

    def act_copy(slot, c):
        source = (half, 0, half)[slot]
        hop = (2, 1, 1)[slot]
        return pltpu.make_async_remote_copy(
            src_ref=sig.at[pl.ds(source + c * chunk, chunk)],
            dst_ref=sbuf.at[pl.ds(slot * half + c * chunk, chunk)],
            send_sem=act_s.at[slot, c], recv_sem=act_r.at[slot, c],
            device_id={"seq": lax.rem(i + hop, n)}, device_id_type=MESH)

    def relay_copy(c):
        return pltpu.make_async_remote_copy(
            src_ref=sbuf.at[pl.ds(c * chunk, chunk)],
            dst_ref=sbuf.at[pl.ds(2 * half + c * chunk, chunk)],
            send_sem=act_s.at[2, c], recv_sem=act_r.at[2, c],
            device_id={"seq": partner}, device_id_type=MESH)

    relays = jnp.logical_and(side == 1, i >= 2)

    def relay(c):
        @pl.when(relays)
        def _():
            act_copy(0, c).wait_recv()
            relay_copy(c).start()

    def act_sends(slot):
        if slot == 2:
            return side == 0
        return i + (2, 1)[slot] < n

    def act_wait(slot, c):
        if slot == 0:
            pl.when(jnp.logical_and(side == 0, i >= 2))(act_copy(0, c).wait_recv)
        else:
            pl.when(i >= 1)(act_copy(slot, c).wait_recv)

    def seq_start(l):
        def go(d, _):
            for w in both:
                seq_copy(l, w, d).start()
            return 0
        lax.fori_loop(1, pairs, go, 0)

    def pair_start(l):
        def go(d, _):
            for w in both:
                seq_copy(l, w, d).wait_recv()
            return 0
        lax.fori_loop(1, pairs, go, 0)
        for w in both:
            own_copy(l, w).wait()
        for w in both:
            par_copy(l, w).start()
        for s in range(len(stages)):
            bat_start(l, s, 0, 0)

    stages = [(m, [o for o in range(nb) if all(o & x == 0 or x > m for x in masks)]) for m in masks]

    def bat_start(l, s, index, parity):
        m, held = stages[s]
        for w in both:
            bat_copy(l, w, m, held[index], parity).start()

    def bat_start_other(l):
        for w in both:
            par_copy(l, w).wait_recv()
        for s in range(len(stages)):
            bat_start(l, s, 0, 1)

    def bat_pass(l):
        for s, (m, held) in enumerate(stages):
            for index, o in enumerate(held):
                for parity in range(2):
                    for w in both:
                        bat_copy(l, w, m, o, parity).wait_recv()
                    for later in range(s + 1, len(stages)):
                        bat_start(l, later, stages[later][1].index(o + m), parity)

    for l in range(layers):
        for w in both:
            own_copy(l, w).start()
    if not gather_blend:
        blend = pltpu.make_async_copy(bw, bfull, own_sem.at[0, 1])
        blend.start()

    pl.semaphore_wait(barrier, n - 1 + len(masks))
    seq_start(0)
    for slot in (0, 2, 1):
        @pl.when(act_sends(slot))
        def _():
            for c in range(CHUNKS):
                act_copy(slot, c).start()

    @pl.when(i == 0)
    def _():
        sbuf[pl.ds(half, rows), :] = jnp.zeros((rows, channels), sbuf.dtype)

    @pl.when(i < 2)
    def _():
        sbuf[pl.ds(0, half), :] = jnp.zeros((half, channels), sbuf.dtype)

    seq_start(1)

    def layer(l, src, dst, shift, start, c):
        kernel_rows = kfull.at[l].reshape(n * kw.shape[1], kfull.shape[-1])
        blend_rows = bfull.at[l].reshape(channels, channels) if gather_blend else bfull.at[l]

        def step(t, _):
            for u in range(2):
                at = pl.multiple_of(start + c * chunk + (2 * t + u) * TILE, TILE)
                now = src[pl.ds(at + shift, TILE), :]
                late = src[pl.ds(at, TILE), :]
                pre = jnp.dot(late, kernel_rows[:channels, :], preferred_element_type=jnp.float32)
                pre += jnp.dot(now, kernel_rows[channels:, :], preferred_element_type=jnp.float32)
                gate = 0.5 * jnp.tanh(0.5 * pre[:, channels:]) + 0.5
                gated = (jnp.tanh(pre[:, :channels]) * gate).astype(jnp.bfloat16)
                mix = jnp.dot(gated, blend_rows[...], preferred_element_type=jnp.float32)
                dst[pl.ds(at, TILE), :] = (now.astype(jnp.float32) + mix).astype(jnp.bfloat16)
            return 0

        lax.fori_loop(0, chunk // (2 * TILE), step, 0)

    done = []

    def write(l, ref, start, c, place):
        copy = pltpu.make_async_copy(
            ref.at[pl.ds(start + c * chunk, chunk)], out.at[l, pl.ds(place * half + c * chunk, chunk)],
            out_sem.at[l, place, c])
        copy.start()
        done.append(copy)

    pair_start(0)
    relay(0)
    bat_start_other(0)
    bat_pass(0)
    load.wait()
    if not gather_blend:
        blend.wait()
    for c in range(CHUNKS):
        layer(0, sbuf, hbuf, half, 3 * half, c)
        write(0, hbuf, 3 * half, c, 1)
        if c == 0:
            for later in range(1, CHUNKS):
                relay(later)
            pair_start(1)
    bat_start_other(1)
    for c in range(CHUNKS):
        act_wait(2, c)
        layer(0, sbuf, hbuf, half, 2 * half, c)
        write(0, hbuf, 2 * half, c, 0)
    bat_pass(1)
    for c in range(CHUNKS):
        act_wait(1, c)
        layer(0, sbuf, hbuf, half, half, c)
        layer(1, hbuf, obuf, rows, half, c)
        write(1, obuf, half, c, 1)
    for c in range(CHUNKS):
        act_wait(0, c)
        layer(0, sbuf, hbuf, half, 0, c)
        layer(1, hbuf, obuf, rows, 0, c)
        write(1, obuf, 0, c, 0)

    def seq_sent(d, _):
        for l in range(layers):
            for w in both:
                seq_copy(l, w, d).wait_send()
        return 0

    lax.fori_loop(1, pairs, seq_sent, 0)
    for l in range(layers):
        for w in both:
            par_copy(l, w).wait_send()
        for m, held in stages:
            for o in held:
                for parity in range(2):
                    for w in both:
                        bat_copy(l, w, m, o, parity).wait_send()
    for slot in range(3):
        @pl.when(act_sends(slot))
        def _():
            for c in range(CHUNKS):
                act_copy(slot, c).wait_send()

    @pl.when(relays)
    def _():
        for c in range(CHUNKS):
            relay_copy(c).wait_send()
    for copy in done:
        copy.wait()


def per_device(n, nb, signal, kernel_weight_stack, blend_weight_stack):
    rows, channels = signal.shape
    layers, part_rows, width = kernel_weight_stack.shape
    gather_blend = blend_weight_stack.shape[1] % 16 == 0
    if not gather_blend:
        blend_weight_stack = lax.all_gather(blend_weight_stack, "seq", axis=1, tiled=True)
    blend_shape = (layers, channels, channels)
    if gather_blend:
        blend_shape = (layers, n // 2, 2, blend_weight_stack.shape[1], channels)
    half = rows // 2
    dma = pltpu.SemaphoreType.DMA
    any_space = pl.BlockSpec(memory_space=pl.ANY)
    return pl.pallas_call(
        functools.partial(kernel, n, nb, gather_blend),
        out_shape=jax.ShapeDtypeStruct((layers, rows, channels), signal.dtype),
        in_specs=[any_space] * 3,
        out_specs=any_space,
        scratch_shapes=[
            pltpu.VMEM((5 * half, channels), signal.dtype),
            pltpu.VMEM((4 * half, channels), signal.dtype),
            pltpu.VMEM((rows, channels), signal.dtype),
            pltpu.VMEM((layers, n // 2, 2, part_rows, width), signal.dtype),
            pltpu.VMEM(blend_shape, signal.dtype),
            dma((layers, 2, n // 2)), dma((layers, 2, n // 2)),
            dma((layers, 2)), dma((layers, 2)),
            dma((layers, 2, nb, 2)), dma((layers, 2, nb, 2)),
            dma((3, CHUNKS)), dma((3, CHUNKS)),
            dma((layers, 2)), dma, dma((layers, 2, CHUNKS)),
        ],
        compiler_params=pltpu.CompilerParams(
            collective_id=0, has_side_effects=True, vmem_limit_bytes=62 * 2**20),
        cost_estimate=pl.CostEstimate(
            flops=3 * 2 * rows * channels * (2 * width + channels),
            bytes_accessed=2 * rows * channels * 2 * 3, transcendentals=3 * rows * width),
    )(signal, kernel_weight_stack, blend_weight_stack)


def solution(mesh):
    return jax.shard_map(
        functools.partial(per_device, mesh.shape["seq"], mesh.shape["batch"]),
        mesh=mesh,
        in_specs=(P(("batch", "seq"), None), P(None, "seq", None), P(None, "seq", None)),
        out_specs=P(None, ("batch", "seq"), None),
        check_vma=False,
    )
```

```python
import functools

import jax
import jax.numpy as jnp
from jax import lax
from jax.experimental import pallas as pl
from jax.experimental.pallas import tpu as pltpu
from jax.sharding import PartitionSpec as P

MESH = pl.DeviceIdType.MESH
TILE = 256
CHUNKS = 2


def flip(index, bit):
    return index + bit - 2 * bit * ((index // bit) % 2)


def kernel(n, nb, gather_blend, sig, kw, bw, out, sbuf, hbuf, obuf, kfull, bfull,
           seq_s, seq_r, par_s, par_r, bat_s, bat_r, act_s, act_r, own_sem, load_sem, out_sem):
    i = lax.axis_index("seq")
    b = lax.axis_index("batch")
    rows = sig.shape[0]
    half = rows // 2
    chunk = half // CHUNKS
    layers = kw.shape[0]
    channels = sig.shape[1]
    masks = [nb >> (k + 1) for k in range(nb.bit_length() - 1)]
    pairs = n // 2
    pair, side = i // 2, i % 2
    partner = flip(i, 1)

    load = pltpu.make_async_copy(sig, sbuf.at[pl.ds(3 * half, rows)], load_sem)
    load.start()

    barrier = pltpu.get_barrier_semaphore()

    def greet(d, _):
        pl.semaphore_signal(barrier, inc=1, device_id={"seq": lax.rem(i + d, n)}, device_id_type=MESH)
        return 0

    lax.fori_loop(1, n, greet, 0)
    for m in masks:
        pl.semaphore_signal(barrier, inc=1, device_id={"batch": flip(b, m)}, device_id_type=MESH)

    weights = [(kw, kfull)] + ([(bw, bfull)] if gather_blend else [])
    both = range(len(weights))

    def cols(full, quarter):
        width = full.shape[-1] // nb
        return pl.ds(pl.multiple_of(quarter * width, width), width)

    def seq_copy(l, w, d):
        part, full = weights[w]
        return pltpu.make_async_remote_copy(
            src_ref=part.at[l, :, cols(full, b)],
            dst_ref=full.at[l, pair, side, :, cols(full, b)],
            send_sem=seq_s.at[l, w, d], recv_sem=seq_r.at[l, w, d],
            device_id={"seq": lax.rem(i + 2 * d, n)}, device_id_type=MESH)

    def own_copy(l, w):
        part, full = weights[w]
        return pltpu.make_async_copy(
            part.at[l, :, cols(full, b)], full.at[l, pair, side, :, cols(full, b)], own_sem.at[l, w])

    def par_copy(l, w):
        part, full = weights[w]
        where = full.at[l, :, side, :, cols(full, b)]
        return pltpu.make_async_remote_copy(
            src_ref=where, dst_ref=where, send_sem=par_s.at[l, w], recv_sem=par_r.at[l, w],
            device_id={"seq": partner}, device_id_type=MESH)

    def bat_copy(l, w, m, o, parity):
        part, full = weights[w]
        quarter = b
        for bit in masks:
            if o & bit:
                quarter = flip(quarter, bit)
        which = lax.rem(side + parity, 2)
        where = full.at[l, :, which, :, cols(full, quarter)]
        return pltpu.make_async_remote_copy(
            src_ref=where, dst_ref=where,
            send_sem=bat_s.at[l, w, o + m, parity], recv_sem=bat_r.at[l, w, o + m, parity],
            device_id={"batch": flip(b, m)}, device_id_type=MESH)

    def act_copy(slot, c):
        source = (half, 0, half)[slot]
        hop = (2, 1, 1)[slot]
        return pltpu.make_async_remote_copy(
            src_ref=sig.at[pl.ds(source + c * chunk, chunk)],
            dst_ref=sbuf.at[pl.ds(slot * half + c * chunk, chunk)],
            send_sem=act_s.at[slot, c], recv_sem=act_r.at[slot, c],
            device_id={"seq": lax.rem(i + hop, n)}, device_id_type=MESH)

    def relay_copy(c):
        return pltpu.make_async_remote_copy(
            src_ref=sbuf.at[pl.ds(c * chunk, chunk)],
            dst_ref=sbuf.at[pl.ds(2 * half + c * chunk, chunk)],
            send_sem=act_s.at[2, c], recv_sem=act_r.at[2, c],
            device_id={"seq": partner}, device_id_type=MESH)

    relays = jnp.logical_and(side == 1, i >= 2)

    def relay(c):
        @pl.when(relays)
        def _():
            act_copy(0, c).wait_recv()
            relay_copy(c).start()

    def act_sends(slot):
        if slot == 2:
            return side == 0
        return i + (2, 1)[slot] < n

    def act_wait(slot, c):
        if slot == 0:
            pl.when(jnp.logical_and(side == 0, i >= 2))(act_copy(0, c).wait_recv)
        else:
            pl.when(i >= 1)(act_copy(slot, c).wait_recv)

    def seq_start(l):
        def go(d, _):
            for w in both:
                seq_copy(l, w, d).start()
            return 0
        lax.fori_loop(1, pairs, go, 0)

    def pair_start(l):
        def go(d, _):
            for w in both:
                seq_copy(l, w, d).wait_recv()
            return 0
        lax.fori_loop(1, pairs, go, 0)
        for w in both:
            own_copy(l, w).wait()
        for w in both:
            par_copy(l, w).start()
        for s in range(len(stages)):
            bat_start(l, s, 0, 0)

    stages = [(m, [o for o in range(nb) if all(o & x == 0 or x > m for x in masks)]) for m in masks]

    def bat_start(l, s, index, parity):
        m, held = stages[s]
        for w in both:
            bat_copy(l, w, m, held[index], parity).start()

    def bat_start_other(l):
        for w in both:
            par_copy(l, w).wait_recv()
        for s in range(len(stages)):
            bat_start(l, s, 0, 1)

    def bat_pass(l):
        for s, (m, held) in enumerate(stages):
            for index, o in enumerate(held):
                for parity in range(2):
                    for w in both:
                        bat_copy(l, w, m, o, parity).wait_recv()
                    for later in range(s + 1, len(stages)):
                        bat_start(l, later, stages[later][1].index(o + m), parity)

    for l in range(layers):
        for w in both:
            own_copy(l, w).start()
    if not gather_blend:
        blend = pltpu.make_async_copy(bw, bfull, own_sem.at[0, 1])
        blend.start()

    pl.semaphore_wait(barrier, n - 1 + len(masks))
    seq_start(0)
    seq_start(1)

    def act_start(slot):
        @pl.when(act_sends(slot))
        def _():
            for c in range(CHUNKS):
                act_copy(slot, c).start()

    @pl.when(i == 0)
    def _():
        sbuf[pl.ds(half, rows), :] = jnp.zeros((rows, channels), sbuf.dtype)

    @pl.when(i < 2)
    def _():
        sbuf[pl.ds(0, half), :] = jnp.zeros((half, channels), sbuf.dtype)

    def layer(l, src, dst, shift, start, c):
        kernel_rows = kfull.at[l].reshape(n * kw.shape[1], kfull.shape[-1])
        blend_rows = bfull.at[l].reshape(channels, channels) if gather_blend else bfull.at[l]

        def step(t, _):
            for u in range(2):
                at = pl.multiple_of(start + c * chunk + (2 * t + u) * TILE, TILE)
                now = src[pl.ds(at + shift, TILE), :]
                late = src[pl.ds(at, TILE), :]
                pre = jnp.dot(late, kernel_rows[:channels, :], preferred_element_type=jnp.float32)
                pre += jnp.dot(now, kernel_rows[channels:, :], preferred_element_type=jnp.float32)
                gate = 0.5 * jnp.tanh(0.5 * pre[:, channels:]) + 0.5
                gated = (jnp.tanh(pre[:, :channels]) * gate).astype(jnp.bfloat16)
                mix = jnp.dot(gated, blend_rows[...], preferred_element_type=jnp.float32)
                dst[pl.ds(at, TILE), :] = (now.astype(jnp.float32) + mix).astype(jnp.bfloat16)
            return 0

        lax.fori_loop(0, chunk // (2 * TILE), step, 0)

    done = []

    def write(l, ref, start, c, place):
        copy = pltpu.make_async_copy(
            ref.at[pl.ds(start + c * chunk, chunk)], out.at[l, pl.ds(place * half + c * chunk, chunk)],
            out_sem.at[l, place, c])
        copy.start()
        done.append(copy)

    pair_start(0)
    act_start(0)
    bat_start_other(0)
    act_start(2)
    act_start(1)
    bat_pass(0)
    relay(0)
    load.wait()
    if not gather_blend:
        blend.wait()
    for c in range(CHUNKS):
        layer(0, sbuf, hbuf, half, 3 * half, c)
        write(0, hbuf, 3 * half, c, 1)
        if c == 0:
            for later in range(1, CHUNKS):
                relay(later)
            pair_start(1)
    bat_start_other(1)
    for c in range(CHUNKS):
        act_wait(2, c)
        layer(0, sbuf, hbuf, half, 2 * half, c)
        write(0, hbuf, 2 * half, c, 0)
    bat_pass(1)
    for c in range(CHUNKS):
        act_wait(1, c)
        layer(0, sbuf, hbuf, half, half, c)
        layer(1, hbuf, obuf, rows, half, c)
        write(1, obuf, half, c, 1)
    for c in range(CHUNKS):
        act_wait(0, c)
        layer(0, sbuf, hbuf, half, 0, c)
        layer(1, hbuf, obuf, rows, 0, c)
        write(1, obuf, 0, c, 0)

    def seq_sent(d, _):
        for l in range(layers):
            for w in both:
                seq_copy(l, w, d).wait_send()
        return 0

    lax.fori_loop(1, pairs, seq_sent, 0)
    for l in range(layers):
        for w in both:
            par_copy(l, w).wait_send()
        for m, held in stages:
            for o in held:
                for parity in range(2):
                    for w in both:
                        bat_copy(l, w, m, o, parity).wait_send()
    for slot in range(3):
        @pl.when(act_sends(slot))
        def _():
            for c in range(CHUNKS):
                act_copy(slot, c).wait_send()

    @pl.when(relays)
    def _():
        for c in range(CHUNKS):
            relay_copy(c).wait_send()
    for copy in done:
        copy.wait()


def per_device(n, nb, signal, kernel_weight_stack, blend_weight_stack):
    rows, channels = signal.shape
    layers, part_rows, width = kernel_weight_stack.shape
    gather_blend = blend_weight_stack.shape[1] % 16 == 0
    if not gather_blend:
        blend_weight_stack = lax.all_gather(blend_weight_stack, "seq", axis=1, tiled=True)
    blend_shape = (layers, channels, channels)
    if gather_blend:
        blend_shape = (layers, n // 2, 2, blend_weight_stack.shape[1], channels)
    half = rows // 2
    dma = pltpu.SemaphoreType.DMA
    any_space = pl.BlockSpec(memory_space=pl.ANY)
    return pl.pallas_call(
        functools.partial(kernel, n, nb, gather_blend),
        out_shape=jax.ShapeDtypeStruct((layers, rows, channels), signal.dtype),
        in_specs=[any_space] * 3,
        out_specs=any_space,
        scratch_shapes=[
            pltpu.VMEM((5 * half, channels), signal.dtype),
            pltpu.VMEM((4 * half, channels), signal.dtype),
            pltpu.VMEM((rows, channels), signal.dtype),
            pltpu.VMEM((layers, n // 2, 2, part_rows, width), signal.dtype),
            pltpu.VMEM(blend_shape, signal.dtype),
            dma((layers, 2, n // 2)), dma((layers, 2, n // 2)),
            dma((layers, 2)), dma((layers, 2)),
            dma((layers, 2, nb, 2)), dma((layers, 2, nb, 2)),
            dma((3, CHUNKS)), dma((3, CHUNKS)),
            dma((layers, 2)), dma, dma((layers, 2, CHUNKS)),
        ],
        compiler_params=pltpu.CompilerParams(
            collective_id=0, has_side_effects=True, vmem_limit_bytes=62 * 2**20),
        cost_estimate=pl.CostEstimate(
            flops=3 * 2 * rows * channels * (2 * width + channels),
            bytes_accessed=2 * rows * channels * 2 * 3, transcendentals=3 * rows * width),
    )(signal, kernel_weight_stack, blend_weight_stack)


def solution(mesh):
    return jax.shard_map(
        functools.partial(per_device, mesh.shape["seq"], mesh.shape["batch"]),
        mesh=mesh,
        in_specs=(P(("batch", "seq"), None), P(None, "seq", None), P(None, "seq", None)),
        out_specs=P(None, ("batch", "seq"), None),
        check_vma=False,
    )
```
